32 devices in a mesh: slab: 16 (over z, y, x), grp: 2 (over core).
Axes of the slice: x: 2, y: 2, z: 4, core: 2. Of those that a mesh axis runs over, the one named last changes fastest.
Arguments:
- ply_masks: int32 [3, 32768], P(None, ('slab', 'grp')), may hold values from 0 to 65535, as said below
- severity: bfloat16 [48, 32768], P(None, ('slab', 'grp')), may hold values from 0.29882812 to 0.8984375
- shape_grads: float32 [8, 32768], P(None, ('slab', 'grp')), may hold values from -4 to 4
- element_area: float32 [32768], P(('slab', 'grp')), may hold values from 0.5 to 2
- displacement: float32 [24, 32768], P(None, ('slab', 'grp')), may hold values from -6 to 6
- ply_stiffness: float32 [8, 48], replicated
- live_counts: int32 [32], P(('slab', 'grp')), may hold values from 1 to 1024, as said below
- connectivity: int32 [4, 32768], P(None, ('slab', 'grp')), may hold values from 0 to 1279, as said below
- interface_slots: int32 [2, 4096], P(None, ('slab', 'grp')), may hold values from 0 to 1023, as said below
- send_rows: int32 [4096], P(('slab', 'grp')), may hold values from 0 to 1023
- seam_rows: int32 [4096], P(('slab', 'grp')), may hold values from 0 to 1023
Outputs:
- assembled: float32 [42, 32768], P(None, ('slab', 'grp'))
The draws below stay inside these ranges and needn't reach their ends.
Inputs may be any that keep to these rules, and one draw needn't show every extreme that they name: `ply_masks`: bit j of word w is the damaged state of ply 16 w + j; the share of damaged plies differs from device to device. `live_counts`: A device uses its element slots 0 up to its count minus one; one device uses all of them. `connectivity`: values are local slots of the element's own device. `interface_slots`: on each device the 256 entries of both lists are distinct element slots.
All inputs are finite; a program needn't handle non-finite values.
Results may differ from the reference program's by a relative error of at most 0.0003.
Values may be sent and summed in bfloat16 or wider, within the bound.
A program may use at most 128 MiB of HBM per device.

```python
import math
import jax
import jax.numpy as jnp
from jax import lax

PLIES = 48
E_DEV = 1024
CAP = 8
SEAM = 128
IF = 128
ELEMS = 32768
LSLOTS = 1280
SEND_ALL = 4096
SEAM_ALL = 4096
N_SLAB = 16
N_GRP = 2


def draw_ply_stiffness(key, part):
    lower = jnp.array([2.0, 0.2, -0.3, 2.0, -0.3, 0.5, 0.3, 0.3], jnp.float32)
    upper = jnp.array([4.0, 0.5, 0.3, 4.0, 0.3, 1.0, 0.6, 0.6], jnp.float32)
    spread = jax.random.uniform(key, (8, PLIES), jnp.float32)
    return lower[:, None] + (upper - lower)[:, None] * spread


def draw_ply_masks(key, part):
    devices = N_SLAB * N_GRP
    first_key, second_key = jax.random.split(key)
    chance = jax.random.randint(first_key, (devices,), 20, 61)
    per_column = jnp.repeat(chance, E_DEV)
    rolls = jax.random.randint(second_key, (3, 16, devices * E_DEV), 0, 100)
    ply_bits = (rolls < per_column[None, None]).astype(jnp.int32)
    powers = 2 ** jnp.arange(16, dtype=jnp.int32)
    words = jnp.sum(ply_bits * powers[None, :, None], axis=1)
    return words.at[0, ::E_DEV].set(2 ** 16 - 1)


def draw_live_counts(key, part):
    devices = N_SLAB * N_GRP
    first_key, second_key = jax.random.split(key)
    counts = jax.random.randint(first_key, (devices,), E_DEV // 4, E_DEV // 2 + 1)
    busiest = jax.random.randint(second_key, (), 0, devices)
    return counts.at[busiest].set(E_DEV)


def draw_connectivity(key, part):
    total = N_SLAB * N_GRP * E_DEV
    shared_end = E_DEV + N_SLAB * CAP
    keys = jax.random.split(key, 7)
    kind = jax.random.randint(keys[0], (4, total), 0, 20)
    own_slot = jax.random.randint(keys[1], (4, total), 0, E_DEV)
    seam_slot = jax.random.randint(keys[3], (4, total), shared_end, shared_end + SEAM)
    own_slab = jnp.arange(total, dtype=jnp.int32) // E_DEV // N_GRP
    side = 2 * jax.random.randint(keys[4], (4, total), 0, 2) - 1
    near_slab = (own_slab[None] + side + N_SLAB) % N_SLAB
    far_slab = jax.random.randint(keys[5], (4, total), 0, N_SLAB)
    pick_near = jax.random.randint(keys[6], (4, total), 0, 3) == 0
    dest_slab = jnp.where(pick_near, near_slab, far_slab)
    within = jax.random.randint(keys[2], (4, total), 0, CAP)
    shared_slot = E_DEV + dest_slab * CAP + within
    return jnp.where(kind < 16, own_slot, jnp.where(kind < 19, shared_slot, seam_slot)).astype(jnp.int32)


def draw_interface_slots(key, part):
    devices = N_SLAB * N_GRP
    keys = jax.random.split(key, devices)
    chosen = jax.vmap(lambda k: jax.random.permutation(k, E_DEV)[:2 * IF])(keys)
    return chosen.reshape(devices, 2, IF).transpose(1, 0, 2).reshape(2, devices * IF).astype(jnp.int32)


def place_ends(result, own_key, least, high):
    place = [jax.random.randint(jax.random.fold_in(own_key, axis), (), 0, length) for axis, length in enumerate(result.shape)]
    main_axis = result.shape.index(max(result.shape))
    next_to = place[:main_axis] + [(place[main_axis] + 1) % result.shape[main_axis]] + place[main_axis + 1:]
    return result.at[tuple(place)].set(least).at[tuple(next_to)].set(high)


def levels(stream_key, extent, cuts, low, high):
    loudness, own = 1.0, jax.random.fold_in(stream_key, 6)
    for position, shards_of in cuts:
        draws = jnp.exp(jax.random.uniform(jax.random.fold_in(own, position), (shards_of,), jnp.float32, low / len(cuts), high / len(cuts)))
        loudness = loudness * jnp.repeat(draws, extent[position] // shards_of).reshape([-1 if axis == position else 1 for axis in range(len(extent))])
    return loudness


def gaussian(rng, extent, deviation, bound, cuts=(), kind=jnp.bfloat16):
    level = levels(rng, extent, cuts, -0.22, 0.18) if cuts else 1.0
    result = jax.random.normal(rng, extent, jnp.float32) * deviation * level
    return jnp.minimum(jnp.maximum(result, -bound), bound).astype(kind)


def setup_inputs(seed: int = 0) -> dict:
    key_of = jax.random.split(jax.random.key(seed), 12)
    return {
        "ply_masks": draw_ply_masks(jax.random.fold_in(key_of[11], 71), 0),
        "severity": jnp.clip(0.29882812 + 0.5996094 * jax.random.uniform(key_of[1], (PLIES, ELEMS), jnp.float32) ** levels(key_of[1], (PLIES, ELEMS), ((1, 32),), -0.2, 0.2), 0.29882812, 0.8984375).astype(jnp.bfloat16),
        "shape_grads": gaussian(key_of[2], (8, ELEMS), 1.0, 4.0, ((1, 32),), jnp.float32),
        "element_area": jnp.clip(jnp.exp(math.log(2.0) - 1.3862944 * jax.random.uniform(key_of[3], (ELEMS,), jnp.float32) ** levels(key_of[3], (ELEMS,), ((0, 32),), -0.2, 0.2)), 0.5, 2.0),
        "displacement": gaussian(key_of[4], (24, ELEMS), 1.0, 6.0, ((1, 32),), jnp.float32),
        "ply_stiffness": draw_ply_stiffness(jax.random.fold_in(key_of[11], 71), 0),
        "live_counts": draw_live_counts(jax.random.fold_in(key_of[11], 71), 0),
        "connectivity": draw_connectivity(jax.random.fold_in(key_of[11], 71), 0),
        "interface_slots": draw_interface_slots(jax.random.fold_in(key_of[11], 71), 0),
        "send_rows": place_ends(jax.random.randint(key_of[9], (SEND_ALL,), 0, E_DEV), jax.random.fold_in(key_of[9], 1), 0, E_DEV - 1).astype(jnp.int32),
        "seam_rows": place_ends(jax.random.randint(key_of[10], (SEAM_ALL,), 0, E_DEV), jax.random.fold_in(key_of[10], 1), 0, E_DEV - 1).astype(jnp.int32),
    }


drill_factor = 0.1
shear_factor = 5.0 / 6.0


def damage_values(ply_masks, severity):
    ply_count = severity.shape[0]
    powers = 2 ** jnp.arange(16, dtype=jnp.int32)
    ply_bits = (ply_masks[:, None, :] // powers[None, :, None]) % 2
    ply_bits = ply_bits.reshape(48, -1)[:ply_count]
    return ply_bits.astype(jnp.float32) * severity.astype(jnp.float32)


def ply_table(ply_stiffness):
    ply_count = ply_stiffness.shape[1]
    thickness = 1.0 / ply_count
    centre = -0.5 + thickness * (jnp.arange(ply_count, dtype=jnp.float32) + 0.5)
    moment_zero = thickness * jnp.ones_like(centre)
    moment_one = thickness * centre
    moment_two = thickness * centre * centre + thickness ** 3 / 12.0
    pieces = [ply_stiffness[0:6] * moment_zero[None], ply_stiffness[0:6] * moment_one[None],
              ply_stiffness[0:6] * moment_two[None], ply_stiffness[6:8] * (shear_factor * moment_zero)[None]]
    return jnp.concatenate(pieces, axis=0)


def symmetric(c):
    return [[c[0], c[1], c[2]], [c[1], c[3], c[4]], [c[2], c[4], c[5]]]


def stiffness(laminate):
    nothing = jnp.zeros_like(laminate[0])
    membrane = symmetric(laminate[0:6])
    coupling = symmetric(laminate[6:12])
    bending = symmetric(laminate[12:18])
    matrix_rows = []
    for i in range(3):
        matrix_rows.append(membrane[i] + coupling[i] + [nothing] * 3)
    for i in range(3):
        matrix_rows.append(coupling[i] + bending[i] + [nothing] * 3)
    matrix_rows.append([nothing] * 6 + [laminate[19], nothing, nothing])
    matrix_rows.append([nothing] * 6 + [nothing, laminate[18], nothing])
    matrix_rows.append([nothing] * 8 + [drill_factor * laminate[5]])
    return jnp.stack([jnp.stack(r, 0) for r in matrix_rows], 0)


def strain_map(shape_grads):
    nothing = jnp.zeros_like(shape_grads[0])
    quarter = 0.25 * jnp.ones_like(shape_grads[0])
    corners = []
    for node in range(4):
        grad_x = shape_grads[2 * node]
        grad_y = shape_grads[2 * node + 1]
        matrix_rows = [
            [grad_x, nothing, nothing, nothing, nothing, nothing],
            [nothing, grad_y, nothing, nothing, nothing, nothing],
            [grad_y, grad_x, nothing, nothing, nothing, nothing],
            [nothing, nothing, nothing, nothing, grad_x, nothing],
            [nothing, nothing, nothing, -grad_y, nothing, nothing],
            [nothing, nothing, nothing, -grad_x, grad_y, nothing],
            [nothing, nothing, grad_x, nothing, quarter, nothing],
            [nothing, nothing, grad_y, -quarter, nothing, nothing],
            [0.5 * grad_y, -0.5 * grad_x, nothing, nothing, nothing, quarter]]
        corners.append(jnp.stack([jnp.stack(r, 0) for r in matrix_rows], 0))
    return jnp.stack(corners, 0)


def element_terms(factors, shape_grads, element_area, displacement, ply_weights):
    highest = lax.Precision.HIGHEST
    n = factors.shape[1]
    laminate = jnp.dot(ply_weights, factors, precision=highest, preferred_element_type=jnp.float32)
    constitutive = stiffness(laminate)
    mapping = strain_map(shape_grads)
    strain = jnp.einsum('aijn,ajn->in', mapping, displacement.reshape(4, 6, n), precision=highest)
    stress = jnp.einsum('ijn,jn->in', constitutive, strain, precision=highest)
    nodal_force = element_area[None, None] * jnp.einsum('aijn,in->ajn', mapping, stress, precision=highest)
    stiff_map = jnp.einsum('ijn,ajkn->aikn', constitutive, mapping, precision=highest)
    blocks = element_area[None, None, None] * jnp.einsum('aijn,aikn->ajkn', mapping, stiff_map, precision=highest)
    return jnp.concatenate([blocks.reshape(4, 36, n), nodal_force], axis=1).reshape(168, n)


def reference(ply_masks, severity, shape_grads, element_area, displacement, ply_stiffness, live_counts, connectivity, interface_slots, send_rows, seam_rows):
    devices = N_SLAB * N_GRP
    damage = damage_values(ply_masks, severity)
    damage_dev = damage.reshape(PLIES, devices, E_DEV).transpose(1, 0, 2)
    pair_lists = interface_slots.reshape(2, devices, IF).transpose(1, 0, 2)
    picked = jax.vmap(lambda w, l: w[:, l])(damage_dev, pair_lists)
    picked = picked.astype(jnp.bfloat16).astype(jnp.float32)
    picked_grid = picked.reshape(N_SLAB, N_GRP, PLIES, 2, IF)
    zero_row = jnp.zeros_like(picked_grid[:1])
    from_prev = jnp.concatenate([zero_row, picked_grid[:-1]], 0)[:, :, :, 1].reshape(devices, PLIES, IF)
    from_next = jnp.concatenate([picked_grid[1:], zero_row], 0)[:, :, :, 0].reshape(devices, PLIES, IF)

    def settle(w, l, p, q):
        d = w.at[:, l[0]].set(0.5 * (w[:, l[0]] + p))
        d = d.at[:, l[1]].set(0.5 * (w[:, l[1]] + q))
        return 1.0 - d

    factors = jax.vmap(settle)(damage_dev, pair_lists, from_prev, from_next)
    ply_weights = ply_table(ply_stiffness)
    grads_dev = shape_grads.reshape(8, devices, E_DEV).transpose(1, 0, 2)
    area_dev = element_area.reshape(devices, E_DEV)
    disp_dev = displacement.reshape(24, devices, E_DEV).transpose(1, 0, 2)
    conn_dev = connectivity.reshape(4, devices, E_DEV).transpose(1, 0, 2)
    column = jnp.arange(E_DEV, dtype=jnp.int32)

    def per_device(items):
        factor_part, grad_part, area_part, disp_part, live_part, conn_part = items
        element_rows = element_terms(factor_part, grad_part, area_part, disp_part, ply_weights)
        element_rows = jnp.where(column[None] < live_part, element_rows, 0.0)
        slot_values = element_rows.reshape(4, 42, E_DEV).transpose(1, 0, 2).reshape(42, 4 * E_DEV)
        return jnp.zeros((42, LSLOTS), jnp.float32).at[:, conn_part.reshape(-1)].add(slot_values)

    slot_sums = lax.map(per_device, (factors, grads_dev, area_dev, disp_dev, live_counts, conn_dev))
    dev_ids = jnp.arange(devices, dtype=jnp.int32)
    slab_of = dev_ids // N_GRP
    grp_of = dev_ids % N_GRP
    own_ids = dev_ids[:, None] * E_DEV + jnp.arange(E_DEV, dtype=jnp.int32)[None]
    dest_slab = jnp.arange(N_SLAB, dtype=jnp.int32)
    shared_rows = send_rows.reshape(devices, N_SLAB, CAP)
    shared_ids = ((dest_slab[None, :, None] * N_GRP + grp_of[:, None, None]) * E_DEV + shared_rows).reshape(devices, N_SLAB * CAP)
    seam_ids = (slab_of * N_GRP + (grp_of + 1) % N_GRP)[:, None] * E_DEV + seam_rows.reshape(devices, SEAM)
    global_ids = jnp.concatenate([own_ids, shared_ids, seam_ids], axis=1).astype(jnp.int32)
    slot_values = slot_sums.transpose(1, 0, 2).reshape(42, devices * LSLOTS)
    return jnp.zeros((42, devices * E_DEV), jnp.float32).at[:, global_ids.reshape(-1)].add(slot_values)
```

```python
import functools

import jax
import jax.numpy as jnp
from jax import lax
from jax.experimental import pallas as pl
from jax.experimental.pallas import tpu as pltpu
from jax.sharding import PartitionSpec as P

MESH = pl.DeviceIdType.MESH
NT = (((1,), (1,)), ((), ()))
NN = (((1,), (0,)), ((), ()))
ROWS = 24
ID_ROW = 22
LO = 256

PAIRS = {
    (0, 0): 0, (0, 1): 1, (1, 1): 2, (0, 3): 3, (0, 4): 4, (1, 3): 5, (1, 4): 6, (0, 5): 7,
    (1, 5): 8, (2, 2): 9, (2, 3): 10, (2, 4): 11, (3, 3): 12, (3, 4): 13, (4, 4): 14, (5, 5): 15,
}


def dot(a, b, dims):
    return lax.dot_general(a, b, dims, preferred_element_type=jnp.float32)


def pair(x):
    high = x.astype(jnp.bfloat16).astype(jnp.float32)
    return jnp.concatenate([high, x - high], axis=0)


def unpair(x):
    return x[:ROWS] + x[ROWS:]


def symmetric(c, at):
    r = [c[at + i : at + i + 1] for i in range(6)]
    return [[r[0], r[1], r[2]], [r[1], r[3], r[4]], [r[2], r[4], r[5]]]


def kernel(
    n_slab, n_grp, masks_ref, sev_ref, grads_ref, area_ref, disp_ref, stiff_ref, live_ref,
    conn_ref, face_ref, send_rows_ref, seam_rows_ref, out_ref,
    near_out, near_in, vals, spread, send_buf, recv_buf, seam_out, seam_in,
    near_send, near_recv, send_sem, recv_sem, seam_send, seam_recv,
):
    f32, bf16, i32 = jnp.float32, jnp.bfloat16, jnp.int32
    s, g = lax.axis_index("slab"), lax.axis_index("grp")
    n = masks_ref.shape[1]
    cap = send_rows_ref.shape[1] // n_slab
    shared = n_slab * cap
    seam = seam_rows_ref.shape[1]
    plies = sev_ref.shape[0]
    groups = n // LO
    rest = -(-(shared + seam) // LO)
    faces = face_ref.shape[1]
    next_grp = lax.rem(g + 1, n_grp)
    prev_grp = lax.rem(g + n_grp - 1, n_grp)

    barrier = pltpu.get_barrier_semaphore()
    for k in range(1, n_slab):
        pl.semaphore_signal(
            barrier, inc=1, device_id=(lax.rem(s + k, n_slab), g), device_id_type=MESH
        )
    around = (next_grp,) if n_grp == 2 else (next_grp, prev_grp)
    for other in around:
        pl.semaphore_signal(barrier, inc=1, device_id=(s, other), device_id_type=MESH)

    parts = []
    for w in range(plies // 16):
        word = jnp.broadcast_to(masks_ref[w : w + 1, :], (16, n))
        parts.append((word >> lax.broadcasted_iota(i32, (16, n), 0)) & 1)
    damage = jnp.concatenate(parts, axis=0).astype(f32) * sev_ref[...].astype(f32)
    face = jnp.concatenate([face_ref[0:1, :], face_ref[1:2, :]], axis=1)
    onface = (lax.broadcasted_iota(i32, (n, 2 * faces), 0) == face).astype(f32).astype(bf16)
    chosen = dot(damage.astype(bf16), onface, NN).astype(bf16)
    near_out[0] = chosen[:, :faces]
    near_out[1] = chosen[:, faces:]

    pl.semaphore_wait(barrier, n_slab - 1 + len(around))

    to_prev = pltpu.make_async_remote_copy(
        src_ref=near_out.at[0], dst_ref=near_in.at[1], send_sem=near_send.at[0],
        recv_sem=near_recv.at[1], device_id=(lax.max(s - 1, 0), g), device_id_type=MESH,
    )
    to_next = pltpu.make_async_remote_copy(
        src_ref=near_out.at[1], dst_ref=near_in.at[0], send_sem=near_send.at[1],
        recv_sem=near_recv.at[0], device_id=(lax.min(s + 1, n_slab - 1), g), device_id_type=MESH,
    )

    @pl.when(s > 0)
    def _():
        to_prev.start()

    @pl.when(s < n_slab - 1)
    def _():
        to_next.start()

    @pl.when(s == 0)
    def _():
        near_in[0] = jnp.zeros((plies, faces), bf16)

    @pl.when(s == n_slab - 1)
    def _():
        near_in[1] = jnp.zeros((plies, faces), bf16)

    stiff = stiff_ref[...]
    h = 1.0 / plies
    z = -0.5 + h * (lax.broadcasted_iota(i32, (8, plies), 1).astype(f32) + 0.5)
    row8 = lax.broadcasted_iota(i32, (8, plies), 0)
    weights = jnp.concatenate(
        [
            stiff * jnp.where(row8 < 6, h, 5.0 / 6.0 * h),
            stiff * (h * z),
            stiff * (h * z * z + h**3 / 12.0),
        ],
        axis=0,
    )
    w1 = weights.astype(bf16).astype(f32)
    w2 = (weights - w1).astype(bf16).astype(f32)
    w3 = weights - w1 - w2
    wcat = jnp.concatenate([w1, w2, w3], axis=0).astype(bf16)
    total = jnp.sum(weights, axis=1, keepdims=True)
    facing = dot(jnp.ones((16, 2 * faces), bf16), onface, NT)[0:1]
    own = dot(wcat, (damage * (1.0 - 0.5 * facing)).astype(bf16), NN)
    own = total - (own[0:24] + own[24:48] + own[48:72])

    low_row = lax.broadcasted_iota(i32, (LO, n), 0)
    for a in range(4):
        low = conn_ref[a : a + 1, :] & (LO - 1)
        spread[a] = (low_row == low).astype(f32).astype(bf16)

    def corners(ref, first, step):
        return jnp.concatenate([ref[first + step * a : first + step * a + 1, :] for a in range(4)], axis=0)

    gx, gy = corners(grads_ref, 0, 2), corners(grads_ref, 1, 2)
    u, v, w, tx, ty, tz = [corners(disp_ref, i, 6) for i in range(6)]
    strain = [
        jnp.sum(t, axis=0, keepdims=True)
        for t in (
            gx * u, gy * v, gy * u + gx * v, gx * ty, -gy * tx, gy * ty - gx * tx,
            gx * w + 0.25 * ty, gy * w - 0.25 * tx, 0.25 * tz - 0.5 * (gx * v - gy * u),
        )
    ]
    column = lax.broadcasted_iota(i32, (1, n), 1)
    area = jnp.where(column < live_ref[0], area_ref[...], 0.0)

    @pl.when(s > 0)
    def _():
        to_prev.wait_send()
        to_next.wait_recv()

    @pl.when(s < n_slab - 1)
    def _():
        to_next.wait_send()
        to_prev.wait_recv()

    partner = jnp.concatenate([near_in[0], near_in[1]], axis=1)
    partner = 0.5 * dot(partner, onface, NT)
    other = dot(wcat, partner.astype(bf16), NN)
    lam = area * (own - (other[0:24] + other[24:48] + other[48:72]))

    A, B, D = symmetric(lam, 0), symmetric(lam, 8), symmetric(lam, 16)
    sx, sy, sd = lam[7:8], lam[6:7], 0.1 * lam[5:6]
    e = strain
    stress = [A[i][0] * e[0] + A[i][1] * e[1] + A[i][2] * e[2]
              + B[i][0] * e[3] + B[i][1] * e[4] + B[i][2] * e[5] for i in range(3)]
    stress += [B[i][0] * e[0] + B[i][1] * e[1] + B[i][2] * e[2]
               + D[i][0] * e[3] + D[i][1] * e[4] + D[i][2] * e[5] for i in range(3)]
    stress += [sx * e[6], sy * e[7], sd * e[8]]

    def along_u(m):
        return [m[i][0] * gx + m[i][2] * gy for i in range(3)]

    def along_v(m):
        return [m[i][1] * gy + m[i][2] * gx for i in range(3)]

    au, av, bu, bv, du, dv = along_u(A), along_v(A), along_u(B), along_v(B), along_u(D), along_v(D)
    t = stress
    values = [
        gx * au[0] + gy * au[2] + 0.25 * gy * gy * sd,
        gy * au[1] + gx * au[2] - 0.25 * gx * gy * sd,
        gy * av[1] + gx * av[2] + 0.25 * gx * gx * sd,
        -(gy * bu[1] + gx * bu[2]),
        gx * bu[0] + gy * bu[2],
        -(gy * bv[1] + gx * bv[2]),
        gx * bv[0] + gy * bv[2],
        0.125 * gy * sd,
        -0.125 * gx * sd,
        gx * gx * sx + gy * gy * sy,
        -0.25 * gy * sy,
        0.25 * gx * sx,
        gy * dv[1] + gx * dv[2] + 0.0625 * sy,
        -(gx * dv[0] + gy * dv[2]),
        gx * du[0] + gy * du[2] + 0.0625 * sx,
        jnp.broadcast_to(0.0625 * sd, gx.shape),
        gx * t[0] + gy * t[2] + 0.5 * gy * t[8],
        gy * t[1] + gx * t[2] - 0.5 * gx * t[8],
        gx * t[6] + gy * t[7],
        -gy * t[4] - gx * t[5] - 0.25 * t[7],
        gx * t[3] + gy * t[5] + 0.25 * t[6],
        jnp.broadcast_to(0.25 * t[8], gx.shape),
    ]
    nothing = jnp.zeros_like(gx)
    for i, value in enumerate(values + [nothing] * (ROWS - len(values))):
        for a in range(4):
            vals[a, i : i + 1, :] = value[a : a + 1]

    def scattered(first, count):
        total = None
        for a in range(4):
            both = pair(vals[a])
            group = conn_ref[a : a + 1, :] >> 8
            chosen = jnp.concatenate(
                [jnp.where(group == first + i, both, 0.0) for i in range(count)], axis=0
            ).astype(bf16)
            term = dot(chosen, spread[a], NT)
            total = term if total is None else total + term
        return jnp.concatenate(
            [unpair(total[2 * ROWS * i : 2 * ROWS * (i + 1)]) for i in range(count)], axis=1
        )

    sums = scattered(groups, rest)
    row_of = lax.broadcasted_iota(i32, (ROWS, 128), 0)
    for b in range(shared // 128):
        ids = send_rows_ref[:, 128 * b : 128 * (b + 1)].astype(f32)
        block = jnp.where(row_of == ID_ROW, ids, sums[:, 128 * b : 128 * (b + 1)])
        block = jnp.concatenate([block, jnp.zeros((128 - ROWS, 128), f32)], axis=0).T
        send_buf[pl.ds(b * (128 // cap), 128 // cap)] = block.reshape(128 // cap, cap, 128)
    copies = []
    for k in range(1, n_slab):
        to = lax.rem(s + k, n_slab)
        copies.append(
            pltpu.make_async_remote_copy(
                src_ref=send_buf.at[to], dst_ref=recv_buf.at[s], send_sem=send_sem.at[k],
                recv_sem=recv_sem.at[k], device_id=(to, g), device_id_type=MESH,
            )
        )
        copies[-1].start()
    seam_out[...] = jnp.where(
        row_of == ID_ROW, seam_rows_ref[...].astype(f32), sums[:, shared : shared + seam]
    )
    copies.append(
        pltpu.make_async_remote_copy(
            src_ref=seam_out, dst_ref=seam_in, send_sem=seam_send, recv_sem=seam_recv,
            device_id=(s, next_grp), device_id_type=MESH,
        )
    )
    copies[-1].start()
    recv_buf[s] = send_buf[s]

    owned = scattered(0, groups)

    for copy in copies:
        copy.wait()

    row_lane = lax.broadcasted_iota(i32, (128, n), 1)
    for b in range(shared // 128 + 1):
        if b < shared // 128:
            across = recv_buf[pl.ds(b * (128 // cap), 128 // cap)].reshape(128, 128)
            block = across.T[:ROWS]
        else:
            block = seam_in[...]
            across = jnp.concatenate([block, jnp.zeros((128 - ROWS, 128), f32)], axis=0).T
        ids = across[:, ID_ROW : ID_ROW + 1].astype(i32)
        onto = (row_lane == ids).astype(f32).astype(bf16)
        owned = owned + unpair(dot(pair(block).astype(bf16), onto, NN))

    zero = jnp.zeros((1, n), f32)
    for j in range(6):
        for k in range(6):
            at = PAIRS.get((min(j, k), max(j, k)))
            row = 6 * j + k
            out_ref[row : row + 1, :] = zero if at is None else owned[at : at + 1]
    for j in range(6):
        out_ref[36 + j : 37 + j, :] = owned[16 + j : 17 + j]


def on_device(
    n_slab, n_grp, ply_masks, severity, shape_grads, element_area, displacement, ply_stiffness,
    live_counts, connectivity, interface_slots, send_rows, seam_rows,
):
    f32, bf16 = jnp.float32, jnp.bfloat16
    n = ply_masks.shape[1]
    plies = severity.shape[0]
    cap = send_rows.shape[0] // n_slab
    faces = interface_slots.shape[1]
    seam = seam_rows.shape[0]
    vmem = pl.BlockSpec(memory_space=pltpu.VMEM)
    smem = pl.BlockSpec(memory_space=pltpu.SMEM)
    return pl.pallas_call(
        functools.partial(kernel, n_slab, n_grp),
        out_shape=jax.ShapeDtypeStruct((42, n), f32),
        in_specs=[vmem] * 6 + [smem] + [vmem] * 4,
        out_specs=vmem,
        scratch_shapes=[
            pltpu.VMEM((2, plies, faces), bf16),
            pltpu.VMEM((2, plies, faces), bf16),
            pltpu.VMEM((4, ROWS, n), f32),
            pltpu.VMEM((4, LO, n), bf16),
            pltpu.VMEM((n_slab, cap, 128), f32),
            pltpu.VMEM((n_slab, cap, 128), f32),
            pltpu.VMEM((ROWS, seam), f32),
            pltpu.VMEM((ROWS, seam), f32),
            pltpu.SemaphoreType.DMA((2,)),
            pltpu.SemaphoreType.DMA((2,)),
            pltpu.SemaphoreType.DMA((n_slab,)),
            pltpu.SemaphoreType.DMA((n_slab,)),
            pltpu.SemaphoreType.DMA,
            pltpu.SemaphoreType.DMA,
        ],
        compiler_params=pltpu.CompilerParams(
            collective_id=0, has_side_effects=True, vmem_limit_bytes=40 * 1024 * 1024
        ),
    )(
        ply_masks, severity, shape_grads, element_area[None], displacement, ply_stiffness,
        live_counts, connectivity, interface_slots, send_rows[None], seam_rows[None],
    )


def solution(mesh):
    both = ("slab", "grp")
    in_specs = (
        P(None, both), P(None, both), P(None, both), P(both), P(None, both), P(), P(both),
        P(None, both), P(None, both), P(both), P(both),
    )
    return jax.shard_map(
        functools.partial(on_device, mesh.shape["slab"], mesh.shape["grp"]),
        mesh=mesh, in_specs=in_specs, out_specs=P(None, both), check_vma=False,
    )
```

```python
import functools

import jax
import jax.numpy as jnp
from jax import lax
from jax.experimental import pallas as pl
from jax.experimental.pallas import tpu as pltpu
from jax.sharding import PartitionSpec as P

MESH = pl.DeviceIdType.MESH
NT = (((1,), (1,)), ((), ()))
NN = (((1,), (0,)), ((), ()))
ROWS = 24
ID_ROW = 22
LO = 256

PAIRS = {
    (0, 0): 0, (0, 1): 1, (1, 1): 2, (0, 3): 3, (0, 4): 4, (1, 3): 5, (1, 4): 6, (0, 5): 7,
    (1, 5): 8, (2, 2): 9, (2, 3): 10, (2, 4): 11, (3, 3): 12, (3, 4): 13, (4, 4): 14, (5, 5): 15,
}


def dot(a, b, dims):
    return lax.dot_general(a, b, dims, preferred_element_type=jnp.float32)


def pair(x):
    high = x.astype(jnp.bfloat16).astype(jnp.float32)
    return jnp.concatenate([high, x - high], axis=0)


def unpair(x):
    return x[:ROWS] + x[ROWS:]


def symmetric(c, at):
    r = [c[at + i : at + i + 1] for i in range(6)]
    return [[r[0], r[1], r[2]], [r[1], r[3], r[4]], [r[2], r[4], r[5]]]


def kernel(
    n_slab, n_grp, *refs,
):
    inputs, (out_ref,), held, rest = refs[:11], refs[11:12], list(refs[12:22]), refs[22:]
    held.insert(6, inputs[6])
    (
        masks_ref, sev_ref, grads_ref, area_ref, disp_ref, stiff_ref, live_ref,
        conn_ref, face_ref, send_rows_ref, seam_rows_ref,
    ) = held
    (
        load_sem,
        near_out, near_in, vals, spread, send_buf, recv_buf, seam_out, seam_in,
        near_send, near_recv, send_sem, recv_sem, seam_send, seam_recv,
    ) = rest
    loads = {}
    for i in (0, 1, 8, 2, 4, 5, 7, 3, 9, 10):
        loads[i] = pltpu.make_async_copy(inputs[i], held[i], load_sem.at[i])
        loads[i].start()
    f32, bf16, i32 = jnp.float32, jnp.bfloat16, jnp.int32
    s, g = lax.axis_index("slab"), lax.axis_index("grp")
    n = masks_ref.shape[1]
    cap = send_rows_ref.shape[1] // n_slab
    shared = n_slab * cap
    seam = seam_rows_ref.shape[1]
    plies = sev_ref.shape[0]
    groups = n // LO
    beyond = -(-(shared + seam) // LO)
    faces = face_ref.shape[1]
    next_grp = lax.rem(g + 1, n_grp)
    prev_grp = lax.rem(g + n_grp - 1, n_grp)

    barrier = pltpu.get_barrier_semaphore()
    for k in range(1, n_slab):
        pl.semaphore_signal(
            barrier, inc=1, device_id=(lax.rem(s + k, n_slab), g), device_id_type=MESH
        )
    around = (next_grp,) if n_grp == 2 else (next_grp, prev_grp)
    for other in around:
        pl.semaphore_signal(barrier, inc=1, device_id=(s, other), device_id_type=MESH)

    for i in (0, 1, 8):
        loads[i].wait()

    parts = []
    for w in range(plies // 16):
        word = jnp.broadcast_to(masks_ref[w : w + 1, :], (16, n))
        parts.append((word >> lax.broadcasted_iota(i32, (16, n), 0)) & 1)
    damage = jnp.concatenate(parts, axis=0).astype(f32) * sev_ref[...].astype(f32)
    face = jnp.concatenate([face_ref[0:1, :], face_ref[1:2, :]], axis=1)
    onface = (lax.broadcasted_iota(i32, (n, 2 * faces), 0) == face).astype(f32).astype(bf16)
    chosen = dot(damage.astype(bf16), onface, NN).astype(bf16)
    near_out[0] = chosen[:, :faces]
    near_out[1] = chosen[:, faces:]

    pl.semaphore_wait(barrier, n_slab - 1 + len(around))

    to_prev = pltpu.make_async_remote_copy(
        src_ref=near_out.at[0], dst_ref=near_in.at[1], send_sem=near_send.at[0],
        recv_sem=near_recv.at[1], device_id=(lax.max(s - 1, 0), g), device_id_type=MESH,
    )
    to_next = pltpu.make_async_remote_copy(
        src_ref=near_out.at[1], dst_ref=near_in.at[0], send_sem=near_send.at[1],
        recv_sem=near_recv.at[0], device_id=(lax.min(s + 1, n_slab - 1), g), device_id_type=MESH,
    )

    @pl.when(s > 0)
    def _():
        to_prev.start()

    @pl.when(s < n_slab - 1)
    def _():
        to_next.start()

    @pl.when(s == 0)
    def _():
        near_in[0] = jnp.zeros((plies, faces), bf16)

    @pl.when(s == n_slab - 1)
    def _():
        near_in[1] = jnp.zeros((plies, faces), bf16)

    for i in (2, 3, 4, 5, 7, 9, 10):
        loads[i].wait()

    stiff = stiff_ref[...]
    h = 1.0 / plies
    z = -0.5 + h * (lax.broadcasted_iota(i32, (8, plies), 1).astype(f32) + 0.5)
    row8 = lax.broadcasted_iota(i32, (8, plies), 0)
    weights = jnp.concatenate(
        [
            stiff * jnp.where(row8 < 6, h, 5.0 / 6.0 * h),
            stiff * (h * z),
            stiff * (h * z * z + h**3 / 12.0),
        ],
        axis=0,
    )
    w1 = weights.astype(bf16).astype(f32)
    w2 = (weights - w1).astype(bf16).astype(f32)
    w3 = weights - w1 - w2
    wcat = jnp.concatenate([w1, w2, w3], axis=0).astype(bf16)
    total = jnp.sum(weights, axis=1, keepdims=True)
    facing = dot(jnp.ones((16, 2 * faces), bf16), onface, NT)[0:1]
    own = dot(wcat, (damage * (1.0 - 0.5 * facing)).astype(bf16), NN)
    own = total - (own[0:24] + own[24:48] + own[48:72])

    low_row = lax.broadcasted_iota(i32, (LO, n), 0)
    for a in range(4):
        low = conn_ref[a : a + 1, :] & (LO - 1)
        spread[a] = (low_row == low).astype(f32).astype(bf16)

    def corners(ref, first, step):
        return jnp.concatenate([ref[first + step * a : first + step * a + 1, :] for a in range(4)], axis=0)

    gx, gy = corners(grads_ref, 0, 2), corners(grads_ref, 1, 2)
    u, v, w, tx, ty, tz = [corners(disp_ref, i, 6) for i in range(6)]
    strain = [
        jnp.sum(t, axis=0, keepdims=True)
        for t in (
            gx * u, gy * v, gy * u + gx * v, gx * ty, -gy * tx, gy * ty - gx * tx,
            gx * w + 0.25 * ty, gy * w - 0.25 * tx, 0.25 * tz - 0.5 * (gx * v - gy * u),
        )
    ]
    column = lax.broadcasted_iota(i32, (1, n), 1)
    area = jnp.where(column < live_ref[0], area_ref[...], 0.0)

    @pl.when(s > 0)
    def _():
        to_prev.wait_send()
        to_next.wait_recv()

    @pl.when(s < n_slab - 1)
    def _():
        to_next.wait_send()
        to_prev.wait_recv()

    partner = jnp.concatenate([near_in[0], near_in[1]], axis=1)
    partner = 0.5 * dot(partner, onface, NT)
    other = dot(wcat, partner.astype(bf16), NN)
    lam = area * (own - (other[0:24] + other[24:48] + other[48:72]))

    A, B, D = symmetric(lam, 0), symmetric(lam, 8), symmetric(lam, 16)
    sx, sy, sd = lam[7:8], lam[6:7], 0.1 * lam[5:6]
    e = strain
    stress = [A[i][0] * e[0] + A[i][1] * e[1] + A[i][2] * e[2]
              + B[i][0] * e[3] + B[i][1] * e[4] + B[i][2] * e[5] for i in range(3)]
    stress += [B[i][0] * e[0] + B[i][1] * e[1] + B[i][2] * e[2]
               + D[i][0] * e[3] + D[i][1] * e[4] + D[i][2] * e[5] for i in range(3)]
    stress += [sx * e[6], sy * e[7], sd * e[8]]

    def along_u(m):
        return [m[i][0] * gx + m[i][2] * gy for i in range(3)]

    def along_v(m):
        return [m[i][1] * gy + m[i][2] * gx for i in range(3)]

    au, av, bu, bv, du, dv = along_u(A), along_v(A), along_u(B), along_v(B), along_u(D), along_v(D)
    t = stress
    values = [
        gx * au[0] + gy * au[2] + 0.25 * gy * gy * sd,
        gy * au[1] + gx * au[2] - 0.25 * gx * gy * sd,
        gy * av[1] + gx * av[2] + 0.25 * gx * gx * sd,
        -(gy * bu[1] + gx * bu[2]),
        gx * bu[0] + gy * bu[2],
        -(gy * bv[1] + gx * bv[2]),
        gx * bv[0] + gy * bv[2],
        0.125 * gy * sd,
        -0.125 * gx * sd,
        gx * gx * sx + gy * gy * sy,
        -0.25 * gy * sy,
        0.25 * gx * sx,
        gy * dv[1] + gx * dv[2] + 0.0625 * sy,
        -(gx * dv[0] + gy * dv[2]),
        gx * du[0] + gy * du[2] + 0.0625 * sx,
        jnp.broadcast_to(0.0625 * sd, gx.shape),
        gx * t[0] + gy * t[2] + 0.5 * gy * t[8],
        gy * t[1] + gx * t[2] - 0.5 * gx * t[8],
        gx * t[6] + gy * t[7],
        -gy * t[4] - gx * t[5] - 0.25 * t[7],
        gx * t[3] + gy * t[5] + 0.25 * t[6],
        jnp.broadcast_to(0.25 * t[8], gx.shape),
    ]
    nothing = jnp.zeros_like(gx)
    for i, value in enumerate(values + [nothing] * (ROWS - len(values))):
        for a in range(4):
            vals[a, i : i + 1, :] = value[a : a + 1]

    def scattered(first, count):
        total = None
        for a in range(4):
            both = pair(vals[a])
            group = conn_ref[a : a + 1, :] >> 8
            chosen = jnp.concatenate(
                [jnp.where(group == first + i, both, 0.0) for i in range(count)], axis=0
            ).astype(bf16)
            term = dot(chosen, spread[a], NT)
            total = term if total is None else total + term
        return jnp.concatenate(
            [unpair(total[2 * ROWS * i : 2 * ROWS * (i + 1)]) for i in range(count)], axis=1
        )

    sums = scattered(groups, beyond)
    row_of = lax.broadcasted_iota(i32, (ROWS, 128), 0)
    for b in range(shared // 128):
        ids = send_rows_ref[:, 128 * b : 128 * (b + 1)].astype(f32)
        block = jnp.where(row_of == ID_ROW, ids, sums[:, 128 * b : 128 * (b + 1)])
        block = jnp.concatenate([block, jnp.zeros((128 - ROWS, 128), f32)], axis=0).T
        send_buf[pl.ds(b * (128 // cap), 128 // cap)] = block.reshape(128 // cap, cap, 128)
    copies = []
    for k in range(1, n_slab):
        to = lax.rem(s + k, n_slab)
        copies.append(
            pltpu.make_async_remote_copy(
                src_ref=send_buf.at[to], dst_ref=recv_buf.at[s], send_sem=send_sem.at[k],
                recv_sem=recv_sem.at[k], device_id=(to, g), device_id_type=MESH,
            )
        )
        copies[-1].start()
    seam_out[...] = jnp.where(
        row_of == ID_ROW, seam_rows_ref[...].astype(f32), sums[:, shared : shared + seam]
    )
    copies.append(
        pltpu.make_async_remote_copy(
            src_ref=seam_out, dst_ref=seam_in, send_sem=seam_send, recv_sem=seam_recv,
            device_id=(s, next_grp), device_id_type=MESH,
        )
    )
    copies[-1].start()
    recv_buf[s] = send_buf[s]

    owned = scattered(0, groups)

    for copy in copies:
        copy.wait()

    row_lane = lax.broadcasted_iota(i32, (128, n), 1)
    for b in range(shared // 128 + 1):
        if b < shared // 128:
            across = recv_buf[pl.ds(b * (128 // cap), 128 // cap)].reshape(128, 128)
            block = across.T[:ROWS]
        else:
            block = seam_in[...]
            across = jnp.concatenate([block, jnp.zeros((128 - ROWS, 128), f32)], axis=0).T
        ids = across[:, ID_ROW : ID_ROW + 1].astype(i32)
        onto = (row_lane == ids).astype(f32).astype(bf16)
        owned = owned + unpair(dot(pair(block).astype(bf16), onto, NN))

    zero = jnp.zeros((1, n), f32)
    for j in range(6):
        for k in range(6):
            at = PAIRS.get((min(j, k), max(j, k)))
            row = 6 * j + k
            out_ref[row : row + 1, :] = zero if at is None else owned[at : at + 1]
    for j in range(6):
        out_ref[36 + j : 37 + j, :] = owned[16 + j : 17 + j]


def on_device(
    n_slab, n_grp, ply_masks, severity, shape_grads, element_area, displacement, ply_stiffness,
    live_counts, connectivity, interface_slots, send_rows, seam_rows,
):
    f32, bf16 = jnp.float32, jnp.bfloat16
    n = ply_masks.shape[1]
    plies = severity.shape[0]
    cap = send_rows.shape[0] // n_slab
    faces = interface_slots.shape[1]
    seam = seam_rows.shape[0]
    arrays = (
        ply_masks, severity, shape_grads, element_area[None], displacement, ply_stiffness,
        live_counts, connectivity, interface_slots, send_rows[None], seam_rows[None],
    )
    hbm = pl.BlockSpec(memory_space=pltpu.HBM)
    held = [pltpu.VMEM(a.shape, a.dtype) for a in arrays]
    held = held[:6] + held[7:]
    return pl.pallas_call(
        functools.partial(kernel, n_slab, n_grp),
        out_shape=jax.ShapeDtypeStruct((42, n), f32),
        in_specs=[hbm] * 6 + [pl.BlockSpec(memory_space=pltpu.SMEM)] + [hbm] * 4,
        out_specs=pl.BlockSpec(memory_space=pltpu.VMEM),
        scratch_shapes=held + [
            pltpu.SemaphoreType.DMA((len(arrays),)),
            pltpu.VMEM((2, plies, faces), bf16),
            pltpu.VMEM((2, plies, faces), bf16),
            pltpu.VMEM((4, ROWS, n), f32),
            pltpu.VMEM((4, LO, n), bf16),
            pltpu.VMEM((n_slab, cap, 128), f32),
            pltpu.VMEM((n_slab, cap, 128), f32),
            pltpu.VMEM((ROWS, seam), f32),
            pltpu.VMEM((ROWS, seam), f32),
            pltpu.SemaphoreType.DMA((2,)),
            pltpu.SemaphoreType.DMA((2,)),
            pltpu.SemaphoreType.DMA((n_slab,)),
            pltpu.SemaphoreType.DMA((n_slab,)),
            pltpu.SemaphoreType.DMA,
            pltpu.SemaphoreType.DMA,
        ],
        compiler_params=pltpu.CompilerParams(
            collective_id=0, has_side_effects=True, vmem_limit_bytes=64 * 1024 * 1024
        ),
    )(*arrays)


def solution(mesh):
    both = ("slab", "grp")
    in_specs = (
        P(None, both), P(None, both), P(None, both), P(both), P(None, both), P(), P(both),
        P(None, both), P(None, both), P(both), P(both),
    )
    return jax.shard_map(
        functools.partial(on_device, mesh.shape["slab"], mesh.shape["grp"]),
        mesh=mesh, in_specs=in_specs, out_specs=P(None, both), check_vma=False,
    )
```

```python
import functools

import jax
import jax.numpy as jnp
from jax import lax
from jax.experimental import pallas as pl
from jax.experimental.pallas import tpu as pltpu
from jax.sharding import PartitionSpec as P

MESH = pl.DeviceIdType.MESH
NT = (((1,), (1,)), ((), ()))
NN = (((1,), (0,)), ((), ()))
ROWS = 24
ID_ROW = 22
LO = 256

PAIRS = {
    (0, 0): 0, (0, 1): 1, (1, 1): 2, (0, 3): 3, (0, 4): 4, (1, 3): 5, (1, 4): 6, (0, 5): 7,
    (1, 5): 8, (2, 2): 9, (2, 3): 10, (2, 4): 11, (3, 3): 12, (3, 4): 13, (4, 4): 14, (5, 5): 15,
}


def dot(a, b, dims):
    return lax.dot_general(a, b, dims, preferred_element_type=jnp.float32)


def pair(x):
    high = x.astype(jnp.bfloat16).astype(jnp.float32)
    return jnp.concatenate([high, x - high], axis=0)


def unpair(x):
    return x[:ROWS] + x[ROWS:]


def symmetric(c, at):
    r = [c[at + i : at + i + 1] for i in range(6)]
    return [[r[0], r[1], r[2]], [r[1], r[3], r[4]], [r[2], r[4], r[5]]]


def fill(vals, gx, gy, strain, lam):
    A, B, D = symmetric(lam, 0), symmetric(lam, 8), symmetric(lam, 16)
    sx, sy, sd = lam[7:8], lam[6:7], 0.1 * lam[5:6]
    e = strain
    stress = [A[i][0] * e[0] + A[i][1] * e[1] + A[i][2] * e[2]
              + B[i][0] * e[3] + B[i][1] * e[4] + B[i][2] * e[5] for i in range(3)]
    stress += [B[i][0] * e[0] + B[i][1] * e[1] + B[i][2] * e[2]
               + D[i][0] * e[3] + D[i][1] * e[4] + D[i][2] * e[5] for i in range(3)]
    stress += [sx * e[6], sy * e[7], sd * e[8]]

    def along_u(m):
        return [m[i][0] * gx + m[i][2] * gy for i in range(3)]

    def along_v(m):
        return [m[i][1] * gy + m[i][2] * gx for i in range(3)]

    au, av, bu, bv, du, dv = along_u(A), along_v(A), along_u(B), along_v(B), along_u(D), along_v(D)
    t = stress
    values = [
        gx * au[0] + gy * au[2] + 0.25 * gy * gy * sd,
        gy * au[1] + gx * au[2] - 0.25 * gx * gy * sd,
        gy * av[1] + gx * av[2] + 0.25 * gx * gx * sd,
        -(gy * bu[1] + gx * bu[2]),
        gx * bu[0] + gy * bu[2],
        -(gy * bv[1] + gx * bv[2]),
        gx * bv[0] + gy * bv[2],
        0.125 * gy * sd,
        -0.125 * gx * sd,
        gx * gx * sx + gy * gy * sy,
        -0.25 * gy * sy,
        0.25 * gx * sx,
        gy * dv[1] + gx * dv[2] + 0.0625 * sy,
        -(gx * dv[0] + gy * dv[2]),
        gx * du[0] + gy * du[2] + 0.0625 * sx,
        jnp.broadcast_to(0.0625 * sd, gx.shape),
        gx * t[0] + gy * t[2] + 0.5 * gy * t[8],
        gy * t[1] + gx * t[2] - 0.5 * gx * t[8],
        gx * t[6] + gy * t[7],
        -gy * t[4] - gx * t[5] - 0.25 * t[7],
        gx * t[3] + gy * t[5] + 0.25 * t[6],
        jnp.broadcast_to(0.25 * t[8], gx.shape),
    ]
    nothing = jnp.zeros_like(gx)
    for i, value in enumerate(values + [nothing] * (ROWS - len(values))):
        for a in range(4):
            vals[a, i : i + 1, :] = value[a : a + 1]


def scattered(vals, spread, groups_of, first, count):
    total = None
    for a in range(4):
        both = pair(vals[a])
        chosen = jnp.concatenate(
            [jnp.where(groups_of[a] == first + i, both, 0.0) for i in range(count)], axis=0
        ).astype(jnp.bfloat16)
        term = dot(chosen, spread[a], NT)
        total = term if total is None else total + term
    return jnp.concatenate(
        [unpair(total[2 * ROWS * i : 2 * ROWS * (i + 1)]) for i in range(count)], axis=1
    )


def kernel(
    n_slab, n_grp, *refs,
):
    inputs, (out_ref,), held, rest = refs[:11], refs[11:12], list(refs[12:22]), refs[22:]
    held.insert(6, inputs[6])
    (
        masks_ref, sev_ref, grads_ref, area_ref, disp_ref, stiff_ref, live_ref,
        conn_ref, face_ref, send_rows_ref, seam_rows_ref,
    ) = held
    (
        load_sem,
        near_out, near_in, vals, spread, vals_f, spread_f, send_buf, recv_buf, seam_out, seam_in,
        near_send, near_recv, send_sem, recv_sem, seam_send, seam_recv,
    ) = rest
    loads = {}
    for i in (0, 1, 8, 2, 4, 5, 7, 3, 9, 10):
        loads[i] = pltpu.make_async_copy(inputs[i], held[i], load_sem.at[i])
        loads[i].start()
    f32, bf16, i32 = jnp.float32, jnp.bfloat16, jnp.int32
    s, g = lax.axis_index("slab"), lax.axis_index("grp")
    n = masks_ref.shape[1]
    cap = send_rows_ref.shape[1] // n_slab
    shared = n_slab * cap
    seam = seam_rows_ref.shape[1]
    plies = sev_ref.shape[0]
    groups = n // LO
    beyond = -(-(shared + seam) // LO)
    faces = face_ref.shape[1]
    next_grp = lax.rem(g + 1, n_grp)
    prev_grp = lax.rem(g + n_grp - 1, n_grp)

    barrier = pltpu.get_barrier_semaphore()
    for k in range(1, n_slab):
        pl.semaphore_signal(
            barrier, inc=1, device_id=(lax.rem(s + k, n_slab), g), device_id_type=MESH
        )
    around = (next_grp,) if n_grp == 2 else (next_grp, prev_grp)
    for other in around:
        pl.semaphore_signal(barrier, inc=1, device_id=(s, other), device_id_type=MESH)

    for i in (0, 1, 8):
        loads[i].wait()

    parts = []
    for w in range(plies // 16):
        word = jnp.broadcast_to(masks_ref[w : w + 1, :], (16, n))
        parts.append((word >> lax.broadcasted_iota(i32, (16, n), 0)) & 1)
    damage = jnp.concatenate(parts, axis=0).astype(f32) * sev_ref[...].astype(f32)
    face = jnp.concatenate([face_ref[0:1, :], face_ref[1:2, :]], axis=1)
    onface = (lax.broadcasted_iota(i32, (n, 2 * faces), 0) == face).astype(f32).astype(bf16)
    chosen = dot(damage.astype(bf16), onface, NN).astype(bf16)
    near_out[0] = chosen[:, :faces]
    near_out[1] = chosen[:, faces:]

    pl.semaphore_wait(barrier, n_slab - 1 + len(around))

    to_prev = pltpu.make_async_remote_copy(
        src_ref=near_out.at[0], dst_ref=near_in.at[1], send_sem=near_send.at[0],
        recv_sem=near_recv.at[1], device_id=(lax.max(s - 1, 0), g), device_id_type=MESH,
    )
    to_next = pltpu.make_async_remote_copy(
        src_ref=near_out.at[1], dst_ref=near_in.at[0], send_sem=near_send.at[1],
        recv_sem=near_recv.at[0], device_id=(lax.min(s + 1, n_slab - 1), g), device_id_type=MESH,
    )

    @pl.when(s > 0)
    def _():
        to_prev.start()

    @pl.when(s < n_slab - 1)
    def _():
        to_next.start()

    @pl.when(s == 0)
    def _():
        near_in[0] = jnp.zeros((plies, faces), bf16)

    @pl.when(s == n_slab - 1)
    def _():
        near_in[1] = jnp.zeros((plies, faces), bf16)

    for i in (2, 3, 4, 5, 7, 9, 10):
        loads[i].wait()

    stiff = stiff_ref[...]
    h = 1.0 / plies
    z = -0.5 + h * (lax.broadcasted_iota(i32, (8, plies), 1).astype(f32) + 0.5)
    row8 = lax.broadcasted_iota(i32, (8, plies), 0)
    weights = jnp.concatenate(
        [
            stiff * jnp.where(row8 < 6, h, 5.0 / 6.0 * h),
            stiff * (h * z),
            stiff * (h * z * z + h**3 / 12.0),
        ],
        axis=0,
    )
    w1 = weights.astype(bf16).astype(f32)
    w2 = (weights - w1).astype(bf16).astype(f32)
    w3 = weights - w1 - w2
    wcat = jnp.concatenate([w1, w2, w3], axis=0).astype(bf16)
    total = jnp.sum(weights, axis=1, keepdims=True)
    facing = dot(jnp.ones((16, 2 * faces), bf16), onface, NT)[0:1]
    own = dot(wcat, (damage * (1.0 - 0.5 * facing)).astype(bf16), NN)
    own = total - (own[0:24] + own[24:48] + own[48:72])

    def corners(ref, first, step):
        return jnp.concatenate([ref[first + step * a : first + step * a + 1, :] for a in range(4)], axis=0)

    gx, gy = corners(grads_ref, 0, 2), corners(grads_ref, 1, 2)
    u, v, w, tx, ty, tz = [corners(disp_ref, i, 6) for i in range(6)]
    strain = [
        jnp.sum(t, axis=0, keepdims=True)
        for t in (
            gx * u, gy * v, gy * u + gx * v, gx * ty, -gy * tx, gy * ty - gx * tx,
            gx * w + 0.25 * ty, gy * w - 0.25 * tx, 0.25 * tz - 0.5 * (gx * v - gy * u),
        )
    ]
    column = lax.broadcasted_iota(i32, (1, n), 1)
    area = jnp.where(column < live_ref[0], area_ref[...], 0.0)

    low_row = lax.broadcasted_iota(i32, (LO, n), 0)
    for a in range(4):
        low = conn_ref[a : a + 1, :] & (LO - 1)
        spread[a] = (low_row == low).astype(f32).astype(bf16)

    slots = conn_ref[...]
    picked = jnp.concatenate(
        [gx, gy] + strain + [area, jnp.zeros((6, n), f32)], axis=0
    )
    p1 = picked.astype(bf16).astype(f32)
    p2 = (picked - p1).astype(bf16).astype(f32)
    ints = jnp.concatenate([slots & (LO - 1), slots >> 8], axis=0).astype(f32)
    picked = jnp.concatenate([p1, p2, picked - p1 - p2, ints], axis=0).astype(bf16)
    picked = dot(picked, onface, NN)
    low_f = picked[72:76].astype(i32)
    group_f = picked[76:80].astype(i32)
    picked = picked[0:24] + picked[24:48] + picked[48:72]
    gx_f, gy_f, area_f = picked[0:4], picked[4:8], picked[17:18]
    strain_f = [picked[8 + i : 9 + i] for i in range(9)]
    low_row = lax.broadcasted_iota(i32, (LO, 2 * faces), 0)
    for a in range(4):
        spread_f[a] = (low_row == low_f[a : a + 1]).astype(f32).astype(bf16)

    fill(vals, gx, gy, strain, area * own)
    groups_of = [conn_ref[a : a + 1, :] >> 8 for a in range(4)]
    sums = scattered(vals, spread, groups_of, groups, beyond)

    @pl.when(s > 0)
    def _():
        to_prev.wait_send()
        to_next.wait_recv()

    @pl.when(s < n_slab - 1)
    def _():
        to_next.wait_send()
        to_prev.wait_recv()

    partner = jnp.concatenate([near_in[0], near_in[1]], axis=1)
    other = dot(wcat, partner, NN)
    other = (-0.5 * area_f) * (other[0:24] + other[24:48] + other[48:72])
    fill(vals_f, gx_f, gy_f, strain_f, other)
    groups_f = [group_f[a : a + 1] for a in range(4)]
    sums = sums + scattered(vals_f, spread_f, groups_f, groups, beyond)

    row_of = lax.broadcasted_iota(i32, (ROWS, 128), 0)
    for b in range(shared // 128):
        ids = send_rows_ref[:, 128 * b : 128 * (b + 1)].astype(f32)
        block = jnp.where(row_of == ID_ROW, ids, sums[:, 128 * b : 128 * (b + 1)])
        block = jnp.concatenate([block, jnp.zeros((128 - ROWS, 128), f32)], axis=0).T
        send_buf[pl.ds(b * (128 // cap), 128 // cap)] = block.reshape(128 // cap, cap, 128)
    copies = []
    for k in range(1, n_slab):
        to = lax.rem(s + k, n_slab)
        copies.append(
            pltpu.make_async_remote_copy(
                src_ref=send_buf.at[to], dst_ref=recv_buf.at[s], send_sem=send_sem.at[k],
                recv_sem=recv_sem.at[k], device_id=(to, g), device_id_type=MESH,
            )
        )
        copies[-1].start()
    seam_out[...] = jnp.where(
        row_of == ID_ROW, seam_rows_ref[...].astype(f32), sums[:, shared : shared + seam]
    )
    copies.append(
        pltpu.make_async_remote_copy(
            src_ref=seam_out, dst_ref=seam_in, send_sem=seam_send, recv_sem=seam_recv,
            device_id=(s, next_grp), device_id_type=MESH,
        )
    )
    copies[-1].start()
    recv_buf[s] = send_buf[s]

    owned = scattered(vals, spread, groups_of, 0, groups)
    owned = owned + scattered(vals_f, spread_f, groups_f, 0, groups)

    for copy in copies:
        copy.wait()

    row_lane = lax.broadcasted_iota(i32, (128, n), 1)
    for b in range(shared // 128 + 1):
        if b < shared // 128:
            across = recv_buf[pl.ds(b * (128 // cap), 128 // cap)].reshape(128, 128)
            block = across.T[:ROWS]
        else:
            block = seam_in[...]
            across = jnp.concatenate([block, jnp.zeros((128 - ROWS, 128), f32)], axis=0).T
        ids = across[:, ID_ROW : ID_ROW + 1].astype(i32)
        onto = (row_lane == ids).astype(f32).astype(bf16)
        owned = owned + unpair(dot(pair(block).astype(bf16), onto, NN))

    out_ref[...] = owned


def expand(rows_ref, out_ref):
    zero = jnp.zeros((1, rows_ref.shape[1]), jnp.float32)
    for j in range(6):
        for k in range(6):
            at = PAIRS.get((min(j, k), max(j, k)))
            row = 6 * j + k
            out_ref[row : row + 1, :] = zero if at is None else rows_ref[at : at + 1, :]
    for j in range(6):
        out_ref[36 + j : 37 + j, :] = rows_ref[16 + j : 17 + j, :]


def on_device(
    n_slab, n_grp, ply_masks, severity, shape_grads, element_area, displacement, ply_stiffness,
    live_counts, connectivity, interface_slots, send_rows, seam_rows,
):
    f32, bf16 = jnp.float32, jnp.bfloat16
    n = ply_masks.shape[1]
    plies = severity.shape[0]
    cap = send_rows.shape[0] // n_slab
    faces = interface_slots.shape[1]
    seam = seam_rows.shape[0]
    arrays = (
        ply_masks, severity, shape_grads, element_area[None], displacement, ply_stiffness,
        live_counts, connectivity, interface_slots, send_rows[None], seam_rows[None],
    )
    hbm = pl.BlockSpec(memory_space=pltpu.HBM)
    held = [pltpu.VMEM(a.shape, a.dtype) for a in arrays]
    held = held[:6] + held[7:]
    rows = pl.pallas_call(
        functools.partial(kernel, n_slab, n_grp),
        out_shape=jax.ShapeDtypeStruct((ROWS, n), f32),
        in_specs=[hbm] * 6 + [pl.BlockSpec(memory_space=pltpu.SMEM)] + [hbm] * 4,
        out_specs=pl.BlockSpec(memory_space=pltpu.VMEM),
        scratch_shapes=held + [
            pltpu.SemaphoreType.DMA((len(arrays),)),
            pltpu.VMEM((2, plies, faces), bf16),
            pltpu.VMEM((2, plies, faces), bf16),
            pltpu.VMEM((4, ROWS, n), f32),
            pltpu.VMEM((4, LO, n), bf16),
            pltpu.VMEM((4, ROWS, 2 * faces), f32),
            pltpu.VMEM((4, LO, 2 * faces), bf16),
            pltpu.VMEM((n_slab, cap, 128), f32),
            pltpu.VMEM((n_slab, cap, 128), f32),
            pltpu.VMEM((ROWS, seam), f32),
            pltpu.VMEM((ROWS, seam), f32),
            pltpu.SemaphoreType.DMA((2,)),
            pltpu.SemaphoreType.DMA((2,)),
            pltpu.SemaphoreType.DMA((n_slab,)),
            pltpu.SemaphoreType.DMA((n_slab,)),
            pltpu.SemaphoreType.DMA,
            pltpu.SemaphoreType.DMA,
        ],
        compiler_params=pltpu.CompilerParams(
            collective_id=0, has_side_effects=True, vmem_limit_bytes=64 * 1024 * 1024
        ),
    )(*arrays)
    vmem = pl.BlockSpec(memory_space=pltpu.VMEM)
    return pl.pallas_call(
        expand, out_shape=jax.ShapeDtypeStruct((42, n), f32), in_specs=[vmem], out_specs=vmem
    )(rows)


def solution(mesh):
    both = ("slab", "grp")
    in_specs = (
        P(None, both), P(None, both), P(None, both), P(both), P(None, both), P(), P(both),
        P(None, both), P(None, both), P(both), P(both),
    )
    return jax.shard_map(
        functools.partial(on_device, mesh.shape["slab"], mesh.shape["grp"]),
        mesh=mesh, in_specs=in_specs, out_specs=P(None, both), check_vma=False,
    )
```

```python
import functools

import jax
import jax.numpy as jnp
from jax import lax
from jax.experimental import pallas as pl
from jax.experimental.pallas import tpu as pltpu
from jax.sharding import PartitionSpec as P

MESH = pl.DeviceIdType.MESH
NT = (((1,), (1,)), ((), ()))
NN = (((1,), (0,)), ((), ()))
ROWS = 24
ID_ROW = 22
LO = 256

PAIRS = {
    (0, 0): 0, (0, 1): 1, (1, 1): 2, (0, 3): 3, (0, 4): 4, (1, 3): 5, (1, 4): 6, (0, 5): 7,
    (1, 5): 8, (2, 2): 9, (2, 3): 10, (2, 4): 11, (3, 3): 12, (3, 4): 13, (4, 4): 14, (5, 5): 15,
}


def dot(a, b, dims):
    return lax.dot_general(a, b, dims, preferred_element_type=jnp.float32)


def pair(x):
    high = x.astype(jnp.bfloat16).astype(jnp.float32)
    return jnp.concatenate([high, x - high], axis=0)


def unpair(x):
    return x[:ROWS] + x[ROWS:]


def symmetric(c, at):
    r = [c[at + i : at + i + 1] for i in range(6)]
    return [[r[0], r[1], r[2]], [r[1], r[3], r[4]], [r[2], r[4], r[5]]]


def fill(vals, gx, gy, strain, lam):
    A, B, D = symmetric(lam, 0), symmetric(lam, 8), symmetric(lam, 16)
    sx, sy, sd = lam[7:8], lam[6:7], 0.1 * lam[5:6]
    e = strain
    stress = [A[i][0] * e[0] + A[i][1] * e[1] + A[i][2] * e[2]
              + B[i][0] * e[3] + B[i][1] * e[4] + B[i][2] * e[5] for i in range(3)]
    stress += [B[i][0] * e[0] + B[i][1] * e[1] + B[i][2] * e[2]
               + D[i][0] * e[3] + D[i][1] * e[4] + D[i][2] * e[5] for i in range(3)]
    stress += [sx * e[6], sy * e[7], sd * e[8]]

    def along_u(m):
        return [m[i][0] * gx + m[i][2] * gy for i in range(3)]

    def along_v(m):
        return [m[i][1] * gy + m[i][2] * gx for i in range(3)]

    au, av, bu, bv, du, dv = along_u(A), along_v(A), along_u(B), along_v(B), along_u(D), along_v(D)
    t = stress
    values = [
        gx * au[0] + gy * au[2] + 0.25 * gy * gy * sd,
        gy * au[1] + gx * au[2] - 0.25 * gx * gy * sd,
        gy * av[1] + gx * av[2] + 0.25 * gx * gx * sd,
        -(gy * bu[1] + gx * bu[2]),
        gx * bu[0] + gy * bu[2],
        -(gy * bv[1] + gx * bv[2]),
        gx * bv[0] + gy * bv[2],
        0.125 * gy * sd,
        -0.125 * gx * sd,
        gx * gx * sx + gy * gy * sy,
        -0.25 * gy * sy,
        0.25 * gx * sx,
        gy * dv[1] + gx * dv[2] + 0.0625 * sy,
        -(gx * dv[0] + gy * dv[2]),
        gx * du[0] + gy * du[2] + 0.0625 * sx,
        jnp.broadcast_to(0.0625 * sd, gx.shape),
        gx * t[0] + gy * t[2] + 0.5 * gy * t[8],
        gy * t[1] + gx * t[2] - 0.5 * gx * t[8],
        gx * t[6] + gy * t[7],
        -gy * t[4] - gx * t[5] - 0.25 * t[7],
        gx * t[3] + gy * t[5] + 0.25 * t[6],
        jnp.broadcast_to(0.25 * t[8], gx.shape),
    ]
    nothing = jnp.zeros_like(gx)
    for i, value in enumerate(values + [nothing] * (ROWS - len(values))):
        for a in range(4):
            vals[a, i : i + 1, :] = value[a : a + 1]


def scattered(vals, spread, groups_of, first, count):
    total = None
    for a in range(4):
        both = pair(vals[a])
        chosen = jnp.concatenate(
            [jnp.where(groups_of[a] == first + i, both, 0.0) for i in range(count)], axis=0
        ).astype(jnp.bfloat16)
        term = dot(chosen, spread[a], NT)
        total = term if total is None else total + term
    return jnp.concatenate(
        [unpair(total[2 * ROWS * i : 2 * ROWS * (i + 1)]) for i in range(count)], axis=1
    )


def kernel(
    n_slab, n_grp, *refs,
):
    inputs, (out_ref,), held, rest = refs[:11], refs[11:12], list(refs[12:22]), refs[22:]
    held.insert(6, inputs[6])
    (
        masks_ref, sev_ref, grads_ref, area_ref, disp_ref, stiff_ref, live_ref,
        conn_ref, face_ref, send_rows_ref, seam_rows_ref,
    ) = held
    (
        load_sem,
        near_out, near_in, vals, spread, vals_f, spread_f, onface, send_buf, recv_buf, seam_out, seam_in,
        near_send, near_recv, send_sem, recv_sem, seam_send, seam_recv,
    ) = rest
    loads = {}
    for i in (8, 1, 0, 2, 4, 5, 7, 3, 9, 10):
        loads[i] = pltpu.make_async_copy(inputs[i], held[i], load_sem.at[i])
        loads[i].start()
    f32, bf16, i32 = jnp.float32, jnp.bfloat16, jnp.int32
    s, g = lax.axis_index("slab"), lax.axis_index("grp")
    n = masks_ref.shape[1]
    cap = send_rows_ref.shape[1] // n_slab
    shared = n_slab * cap
    seam = seam_rows_ref.shape[1]
    plies = sev_ref.shape[0]
    groups = n // LO
    beyond = -(-(shared + seam) // LO)
    faces = face_ref.shape[1]
    next_grp = lax.rem(g + 1, n_grp)
    prev_grp = lax.rem(g + n_grp - 1, n_grp)

    barrier = pltpu.get_barrier_semaphore()
    for k in range(1, n_slab):
        pl.semaphore_signal(
            barrier, inc=1, device_id=(lax.rem(s + k, n_slab), g), device_id_type=MESH
        )
    around = (next_grp,) if n_grp == 2 else (next_grp, prev_grp)
    for other in around:
        pl.semaphore_signal(barrier, inc=1, device_id=(s, other), device_id_type=MESH)

    loads[8].wait()
    face = jnp.concatenate([face_ref[0:1, :], face_ref[1:2, :]], axis=1)
    onface[...] = (lax.broadcasted_iota(i32, (n, 2 * faces), 0) == face).astype(f32).astype(bf16)
    for i in (0, 1):
        loads[i].wait()

    parts = []
    for w in range(plies // 16):
        word = jnp.broadcast_to(masks_ref[w : w + 1, :], (16, n))
        parts.append((word >> lax.broadcasted_iota(i32, (16, n), 0)) & 1)
    damage = jnp.concatenate(parts, axis=0).astype(f32) * sev_ref[...].astype(f32)
    chosen = dot(damage.astype(bf16), onface[...], NN).astype(bf16)
    near_out[0] = chosen[:, :faces]
    near_out[1] = chosen[:, faces:]

    pl.semaphore_wait(barrier, n_slab - 1 + len(around))

    to_prev = pltpu.make_async_remote_copy(
        src_ref=near_out.at[0], dst_ref=near_in.at[1], send_sem=near_send.at[0],
        recv_sem=near_recv.at[1], device_id=(lax.max(s - 1, 0), g), device_id_type=MESH,
    )
    to_next = pltpu.make_async_remote_copy(
        src_ref=near_out.at[1], dst_ref=near_in.at[0], send_sem=near_send.at[1],
        recv_sem=near_recv.at[0], device_id=(lax.min(s + 1, n_slab - 1), g), device_id_type=MESH,
    )

    @pl.when(s > 0)
    def _():
        to_prev.start()

    @pl.when(s < n_slab - 1)
    def _():
        to_next.start()

    @pl.when(s == 0)
    def _():
        near_in[0] = jnp.zeros((plies, faces), bf16)

    @pl.when(s == n_slab - 1)
    def _():
        near_in[1] = jnp.zeros((plies, faces), bf16)

    for i in (2, 3, 4, 5, 7, 9, 10):
        loads[i].wait()

    stiff = stiff_ref[...]
    h = 1.0 / plies
    z = -0.5 + h * (lax.broadcasted_iota(i32, (8, plies), 1).astype(f32) + 0.5)
    row8 = lax.broadcasted_iota(i32, (8, plies), 0)
    weights = jnp.concatenate(
        [
            stiff * jnp.where(row8 < 6, h, 5.0 / 6.0 * h),
            stiff * (h * z),
            stiff * (h * z * z + h**3 / 12.0),
        ],
        axis=0,
    )
    w1 = weights.astype(bf16).astype(f32)
    w2 = (weights - w1).astype(bf16).astype(f32)
    w3 = weights - w1 - w2
    wcat = jnp.concatenate([w1, w2, w3], axis=0).astype(bf16)
    total = jnp.sum(weights, axis=1, keepdims=True)
    facing = dot(jnp.ones((16, 2 * faces), bf16), onface[...], NT)[0:1]
    own = dot(wcat, (damage * (1.0 - 0.5 * facing)).astype(bf16), NN)
    own = total - (own[0:24] + own[24:48] + own[48:72])

    def corners(ref, first, step):
        return jnp.concatenate([ref[first + step * a : first + step * a + 1, :] for a in range(4)], axis=0)

    gx, gy = corners(grads_ref, 0, 2), corners(grads_ref, 1, 2)
    u, v, w, tx, ty, tz = [corners(disp_ref, i, 6) for i in range(6)]
    strain = [
        jnp.sum(t, axis=0, keepdims=True)
        for t in (
            gx * u, gy * v, gy * u + gx * v, gx * ty, -gy * tx, gy * ty - gx * tx,
            gx * w + 0.25 * ty, gy * w - 0.25 * tx, 0.25 * tz - 0.5 * (gx * v - gy * u),
        )
    ]
    column = lax.broadcasted_iota(i32, (1, n), 1)
    area = jnp.where(column < live_ref[0], area_ref[...], 0.0)

    low_row = lax.broadcasted_iota(i32, (LO, n), 0)
    for a in range(4):
        low = conn_ref[a : a + 1, :] & (LO - 1)
        spread[a] = (low_row == low).astype(f32).astype(bf16)

    slots = conn_ref[...]
    picked = jnp.concatenate(
        [gx, gy] + strain + [area, jnp.zeros((6, n), f32)], axis=0
    )
    p1 = picked.astype(bf16).astype(f32)
    p2 = (picked - p1).astype(bf16).astype(f32)
    ints = jnp.concatenate([slots & (LO - 1), slots >> 8], axis=0).astype(f32)
    picked = jnp.concatenate([p1, p2, picked - p1 - p2, ints], axis=0).astype(bf16)
    picked = dot(picked, onface[...], NN)
    low_f = picked[72:76].astype(i32)
    group_f = picked[76:80].astype(i32)
    picked = picked[0:24] + picked[24:48] + picked[48:72]
    gx_f, gy_f, area_f = picked[0:4], picked[4:8], picked[17:18]
    strain_f = [picked[8 + i : 9 + i] for i in range(9)]
    low_row = lax.broadcasted_iota(i32, (LO, 2 * faces), 0)
    for a in range(4):
        spread_f[a] = (low_row == low_f[a : a + 1]).astype(f32).astype(bf16)

    fill(vals, gx, gy, strain, area * own)
    groups_of = [conn_ref[a : a + 1, :] >> 8 for a in range(4)]
    sums = scattered(vals, spread, groups_of, groups, beyond)

    @pl.when(s > 0)
    def _():
        to_prev.wait_send()
        to_next.wait_recv()

    @pl.when(s < n_slab - 1)
    def _():
        to_next.wait_send()
        to_prev.wait_recv()

    partner = jnp.concatenate([near_in[0], near_in[1]], axis=1)
    other = dot(wcat, partner, NN)
    other = (-0.5 * area_f) * (other[0:24] + other[24:48] + other[48:72])
    fill(vals_f, gx_f, gy_f, strain_f, other)
    groups_f = [group_f[a : a + 1] for a in range(4)]
    sums = sums + scattered(vals_f, spread_f, groups_f, groups, beyond)

    row_of = lax.broadcasted_iota(i32, (ROWS, 128), 0)
    for b in range(shared // 128):
        ids = send_rows_ref[:, 128 * b : 128 * (b + 1)].astype(f32)
        block = jnp.where(row_of == ID_ROW, ids, sums[:, 128 * b : 128 * (b + 1)])
        block = jnp.concatenate([block, jnp.zeros((128 - ROWS, 128), f32)], axis=0).T
        send_buf[pl.ds(b * (128 // cap), 128 // cap)] = block.reshape(128 // cap, cap, 128)
    copies = []
    for k in range(1, n_slab):
        to = lax.rem(s + k, n_slab)
        copies.append(
            pltpu.make_async_remote_copy(
                src_ref=send_buf.at[to], dst_ref=recv_buf.at[s], send_sem=send_sem.at[k],
                recv_sem=recv_sem.at[k], device_id=(to, g), device_id_type=MESH,
            )
        )
        copies[-1].start()
    seam_out[...] = jnp.where(
        row_of == ID_ROW, seam_rows_ref[...].astype(f32), sums[:, shared : shared + seam]
    )
    copies.append(
        pltpu.make_async_remote_copy(
            src_ref=seam_out, dst_ref=seam_in, send_sem=seam_send, recv_sem=seam_recv,
            device_id=(s, next_grp), device_id_type=MESH,
        )
    )
    copies[-1].start()
    recv_buf[s] = send_buf[s]

    owned = scattered(vals, spread, groups_of, 0, groups)
    owned = owned + scattered(vals_f, spread_f, groups_f, 0, groups)

    for copy in copies:
        copy.wait()

    row_lane = lax.broadcasted_iota(i32, (128, n), 1)
    blocks, onto = [], []
    for b in range(shared // 128 + 1):
        if b < shared // 128:
            across = recv_buf[pl.ds(b * (128 // cap), 128 // cap)].reshape(128, 128)
            blocks.append(across.T[:ROWS])
        else:
            blocks.append(seam_in[...])
            across = jnp.concatenate([blocks[-1], jnp.zeros((128 - ROWS, 128), f32)], axis=0).T
        ids = across[:, ID_ROW : ID_ROW + 1].astype(i32)
        onto.append((row_lane == ids).astype(f32).astype(bf16))
    blocks = pair(jnp.concatenate(blocks, axis=1)).astype(bf16)
    owned = owned + unpair(dot(blocks, jnp.concatenate(onto, axis=0), NN))
    out_ref[...] = owned


def expand(rows_ref, out_ref):
    zero = jnp.zeros((1, rows_ref.shape[1]), jnp.float32)
    for j in range(6):
        for k in range(6):
            at = PAIRS.get((min(j, k), max(j, k)))
            row = 6 * j + k
            out_ref[row : row + 1, :] = zero if at is None else rows_ref[at : at + 1, :]
    for j in range(6):
        out_ref[36 + j : 37 + j, :] = rows_ref[16 + j : 17 + j, :]


def on_device(
    n_slab, n_grp, ply_masks, severity, shape_grads, element_area, displacement, ply_stiffness,
    live_counts, connectivity, interface_slots, send_rows, seam_rows,
):
    f32, bf16 = jnp.float32, jnp.bfloat16
    n = ply_masks.shape[1]
    plies = severity.shape[0]
    cap = send_rows.shape[0] // n_slab
    faces = interface_slots.shape[1]
    seam = seam_rows.shape[0]
    arrays = (
        ply_masks, severity, shape_grads, element_area[None], displacement, ply_stiffness,
        live_counts, connectivity, interface_slots, send_rows[None], seam_rows[None],
    )
    hbm = pl.BlockSpec(memory_space=pltpu.HBM)
    held = [pltpu.VMEM(a.shape, a.dtype) for a in arrays]
    held = held[:6] + held[7:]
    rows = pl.pallas_call(
        functools.partial(kernel, n_slab, n_grp),
        out_shape=jax.ShapeDtypeStruct((ROWS, n), f32),
        in_specs=[hbm] * 6 + [pl.BlockSpec(memory_space=pltpu.SMEM)] + [hbm] * 4,
        out_specs=pl.BlockSpec(memory_space=pltpu.VMEM),
        scratch_shapes=held + [
            pltpu.SemaphoreType.DMA((len(arrays),)),
            pltpu.VMEM((2, plies, faces), bf16),
            pltpu.VMEM((2, plies, faces), bf16),
            pltpu.VMEM((4, ROWS, n), f32),
            pltpu.VMEM((4, LO, n), bf16),
            pltpu.VMEM((4, ROWS, 2 * faces), f32),
            pltpu.VMEM((4, LO, 2 * faces), bf16),
            pltpu.VMEM((n, 2 * faces), bf16),
            pltpu.VMEM((n_slab, cap, 128), f32),
            pltpu.VMEM((n_slab, cap, 128), f32),
            pltpu.VMEM((ROWS, seam), f32),
            pltpu.VMEM((ROWS, seam), f32),
            pltpu.SemaphoreType.DMA((2,)),
            pltpu.SemaphoreType.DMA((2,)),
            pltpu.SemaphoreType.DMA((n_slab,)),
            pltpu.SemaphoreType.DMA((n_slab,)),
            pltpu.SemaphoreType.DMA,
            pltpu.SemaphoreType.DMA,
        ],
        compiler_params=pltpu.CompilerParams(
            collective_id=0, has_side_effects=True, vmem_limit_bytes=64 * 1024 * 1024
        ),
    )(*arrays)
    vmem = pl.BlockSpec(memory_space=pltpu.VMEM)
    return pl.pallas_call(
        expand, out_shape=jax.ShapeDtypeStruct((42, n), f32), in_specs=[vmem], out_specs=vmem
    )(rows)


def solution(mesh):
    both = ("slab", "grp")
    in_specs = (
        P(None, both), P(None, both), P(None, both), P(both), P(None, both), P(), P(both),
        P(None, both), P(None, both), P(both), P(both),
    )
    return jax.shard_map(
        functools.partial(on_device, mesh.shape["slab"], mesh.shape["grp"]),
        mesh=mesh, in_specs=in_specs, out_specs=P(None, both), check_vma=False,
    )
```
